256 devices in a mesh: grp: 8 (over y, x_lo), wide: 32 (over x_hi, z, core).
Axes of the slice: x: 4 (x_hi: 2, x_lo: 2; x = x_hi * 2 + x_lo), y: 4, z: 8, core: 2. Of those that a mesh axis runs over, the one named last changes fastest.
Arguments:
- acts: bfloat16 [2, 1024, 6144], P(None, 'grp'), may hold values from -6 to 6
- out_grads: bfloat16 [2, 1024, 12288], P(None, 'grp', 'wide'), may hold values from -0.1875 to 0.1875
- a_factor: float32 [2, 768, 6144], P(None, 'wide', 'grp')
- g_factor: float32 [2, 384, 12288], P(None, 'grp', 'wide')
- ainv_store: bfloat16 [32, 2, 6144, 768], P('wide', None, 'grp')
- a_mask: int32 [2, 48, 6], P(None, 'grp'), may hold values from 0 to 1, as said below
- g_inv: bfloat16 [2, 12288, 384], P(None, 'wide')
- g_mask: int32 [2, 96, 3], P(None, 'wide'), may hold values from 0 to 1, as said below
- owner: int32 [2], replicated, may hold values from 0 to 31
Outputs:
- precond: bfloat16 [2, 6144, 12288], P(None, 'grp', 'wide')
- a_new: float32 [2, 768, 6144], P(None, 'wide', 'grp')
- g_new: float32 [2, 384, 12288], P(None, 'grp', 'wide')
The draws below stay inside these ranges and needn't reach their ends.
Inputs may be any that keep to these rules, and one draw needn't show every extreme that they name: Tiles of 128 features form runs of consecutive tiles that never cross a multiple of 768 features; a_mask[l, i, j] is 1 exactly when tile i and tile (i // q) q + j, q = 6, lie in the same run of layer l. Tiles of 128 output units form runs of consecutive tiles that never cross a multiple of 384; g_mask[l, i, j] is 1 exactly when tile i and tile (i // q) q + j, q = 3, lie in the same run of layer l.
All inputs are finite; a program needn't handle non-finite values.
Results may differ from the reference program's by a relative error of at most 0.0058.
Values may be sent and summed in bfloat16 or wider, within the bound.
No kernel may reach another device: no remote copies, remote signals or barrier semaphores. Data moves between devices by JAX's collectives and lax.ppermute only.
A program may use at most 128 MiB of HBM per device.

```python
import math
import jax
import jax.numpy as jnp
from jax import lax

D = 6144
FW = 12288
TILE = 128
LAYERS = 2
TOKENS = 1024
N_GRP = 8
N_WIDE = 32


def dominant(key, shape, spread):
    rows_axis = len(shape) - 2
    cols = shape[-1]
    noise = jax.random.normal(key, shape, jnp.float32) / math.sqrt(cols)
    row_pos = lax.broadcasted_iota(jnp.int32, shape, rows_axis) % cols
    col_pos = lax.broadcasted_iota(jnp.int32, shape, rows_axis + 1)
    eye = (row_pos == col_pos).astype(jnp.float32)
    row_scale = jnp.exp(spread * jax.random.uniform(jax.random.fold_in(key, 7), shape[:-1] + (1,), jnp.float32))
    return (eye + noise) * row_scale


def factor_normal(key, shape, block, off_scale):
    row_pos = lax.broadcasted_iota(jnp.int32, shape, 1)
    col_pos = lax.broadcasted_iota(jnp.int32, shape, 2) % block
    on_diag = (row_pos == col_pos).astype(jnp.float32)
    diag_value = jax.random.uniform(jax.random.fold_in(key, 5), shape, jnp.float32, 0.5, 1.5)
    off_value = off_scale * jax.random.normal(key, shape, jnp.float32)
    return on_diag * diag_value + (1.0 - on_diag) * off_value


def run_mask(key, layers, tiles_all, tiles_block):
    breaks = jax.random.randint(key, (layers, tiles_all), 0, 2)
    position = jnp.arange(tiles_all, dtype=jnp.int32)
    breaks = jnp.where(position % tiles_block == 0, 1, breaks)
    group = jnp.cumsum(breaks, axis=1)
    first = position // tiles_block * tiles_block
    other = first[:, None] + jnp.arange(tiles_block, dtype=jnp.int32)[None, :]
    partner = jnp.take(group, other, axis=1)
    return (group[:, :, None] == partner).astype(jnp.int32)


def draw_a_factor(key, part):
    key = jax.random.fold_in(key, 23)
    shape = (LAYERS, D // N_GRP, D)
    value = factor_normal(key, shape, D // N_GRP, 1.0 / math.sqrt(TOKENS))
    return value


def draw_g_factor(key, part):
    key = jax.random.fold_in(key, 29)
    shape = (LAYERS, FW // N_WIDE, FW)
    value = factor_normal(key, shape, FW // N_WIDE, 1.0 / math.sqrt(TOKENS))
    return value


def draw_ainv_store(key, part):
    key = jax.random.fold_in(key, 11)
    value = dominant(key, (N_WIDE, LAYERS, D, D // N_GRP), 0.7)
    return value.astype(jnp.bfloat16)


def draw_g_inv(key, part):
    key = jax.random.fold_in(key, 13)
    value = dominant(key, (LAYERS, FW, FW // N_WIDE), 0.7)
    return value.astype(jnp.bfloat16)


def draw_a_mask(key, part):
    key = jax.random.fold_in(key, 17)
    return run_mask(key, LAYERS, D // TILE, D // N_GRP // TILE)


def draw_g_mask(key, part):
    key = jax.random.fold_in(key, 19)
    return run_mask(key, LAYERS, FW // TILE, FW // N_WIDE // TILE)


def shard_levels(key, shape, split, low, top_value):
    gain, own = 1.0, jax.random.fold_in(key, 6)
    for dim, parts in split:
        heights = jnp.exp(jax.random.uniform(jax.random.fold_in(own, dim), (parts,), jnp.float32, low / len(split), top_value / len(split)))
        gain = gain * jnp.repeat(heights, shape[dim] // parts).reshape([-1 if axis == dim else 1 for axis in range(len(shape))])
    return gain


def gaussian(rng, shape, deviation, limit, split=(), kind=jnp.bfloat16):
    drawn = jax.random.normal(rng, shape, jnp.float32) * deviation
    if len(split) > 0:
        drawn = shard_levels(rng, shape, split, -0.22, 0.18) * drawn
    return jnp.clip(drawn, min=-limit, max=limit).astype(kind)


def setup_inputs(seed: int = 0) -> dict:
    arg_keys = jax.random.split(jax.random.key(seed), 10)
    acts = gaussian(arg_keys[0], (LAYERS, TOKENS, D), 1.0, 6.0, ((1, 8),))
    out_grads = gaussian(arg_keys[1], (LAYERS, TOKENS, FW), TOKENS ** -0.5, 0.1875, ((1, 8), (2, 32)))
    a_factor = draw_a_factor(jax.random.fold_in(arg_keys[9], 71), 0)
    g_factor = draw_g_factor(jax.random.fold_in(arg_keys[9], 71), 0)
    ainv_store = draw_ainv_store(jax.random.fold_in(arg_keys[9], 71), 0)
    a_mask = draw_a_mask(jax.random.fold_in(arg_keys[9], 71), 0)
    g_inv = draw_g_inv(jax.random.fold_in(arg_keys[9], 71), 0)
    g_mask = draw_g_mask(jax.random.fold_in(arg_keys[9], 71), 0)
    owner = jax.random.randint(arg_keys[8], (LAYERS,), 0, N_WIDE).astype(jnp.int32)
    return {"acts": acts, "out_grads": out_grads, "a_factor": a_factor, "g_factor": g_factor, "ainv_store": ainv_store, "a_mask": a_mask, "g_inv": g_inv, "g_mask": g_mask, "owner": owner}


decay_rate = 0.9


def expand_tiles(mask, tile):
    lead, rows, cols = mask.shape
    grid = jnp.broadcast_to(mask[:, :, None, :, None], (lead, rows, tile, cols, tile))
    return grid.reshape(lead, rows * tile, cols * tile)


def reference(acts, out_grads, a_factor, g_factor, ainv_store, a_mask, g_inv, g_mask, owner):
    slab = D // N_GRP
    gcol = FW // N_WIDE
    a_tiles = expand_tiles(a_mask, TILE).astype(jnp.bfloat16)
    g_tiles = expand_tiles(g_mask, TILE).astype(jnp.bfloat16)
    precond_list = []
    a_list = []
    g_list = []
    for layer in range(LAYERS):
        inputs = acts[layer]
        grads = out_grads[layer]
        split_in = inputs.astype(jnp.float32).reshape(TOKENS, N_GRP, slab)
        gram_a = jnp.einsum("tsr,tsc->rsc", split_in, split_in) / TOKENS
        a_list.append(decay_rate * a_factor[layer] + (1.0 - decay_rate) * gram_a.reshape(slab, D))
        split_out = grads.astype(jnp.float32).reshape(TOKENS, N_WIDE, gcol)
        gram_g = jnp.einsum("twr,twc->rwc", split_out, split_out)
        g_list.append(decay_rate * g_factor[layer] + (1.0 - decay_rate) * gram_g.reshape(gcol, FW))
        stored = lax.dynamic_index_in_dim(ainv_store, owner[layer], 0, keepdims=False)[layer]
        g_panel = (g_inv[layer] * g_tiles[layer]).astype(jnp.float32).reshape(N_WIDE, gcol, gcol)
        blocks = []
        for block in range(N_GRP):
            lower = block * slab
            weight_grad = jnp.dot(inputs[:, lower:lower + slab].T, grads, preferred_element_type=jnp.float32).astype(jnp.bfloat16)
            a_panel = stored[lower:lower + slab] * a_tiles[layer, lower:lower + slab]
            left = jnp.dot(a_panel, weight_grad, preferred_element_type=jnp.float32).astype(jnp.bfloat16)
            right = jnp.einsum("rwk,wkc->rwc", left.astype(jnp.float32).reshape(slab, N_WIDE, gcol), g_panel)
            blocks.append(right.reshape(slab, FW).astype(jnp.bfloat16))
        precond_list.append(jnp.concatenate(blocks, axis=0))
    return jnp.stack(precond_list), jnp.stack(a_list), jnp.stack(g_list)
```

```python
import jax
import jax.numpy as jnp
from jax import lax
from jax.sharding import Mesh, PartitionSpec as P

TILE = 128
DECAY = 0.9
GRP = ("y", "xl")
CHIP = ("xh", "z")
F32 = jnp.float32


def expand(mask):
    return jnp.repeat(jnp.repeat(mask, TILE, axis=0), TILE, axis=1)


def swap(x):
    return lax.ppermute(x, "core", [(0, 1), (1, 0)])


def gather_grp(x):
    wide = jnp.broadcast_to(x[None], (lax.axis_size(GRP),) + x.shape)
    return lax.all_to_all(wide, GRP, 0, 0, tiled=True)


def shards(acts, out_grads, a_factor, g_factor, ainv_store, a_mask, g_inv, g_mask, owner):
    core = lax.axis_index("core")
    other = 1 - core
    first = core == 0
    grp_at = lax.axis_index(GRP)
    chip_at = lax.axis_index(CHIP)
    groups = lax.axis_size(GRP)
    chips = lax.axis_size(CHIP)
    count = acts.shape[1]
    slab = acts.shape[2] // groups
    gcol = out_grads.shape[2]
    arows = a_factor.shape[1]
    grows = g_factor.shape[1]
    tokens = count * groups

    def mine(x):
        return lax.dynamic_index_in_dim(x, core, 0, keepdims=False)

    def theirs(x):
        return lax.dynamic_index_in_dim(x, other, 0, keepdims=False)

    src = mine(owner)
    store = ainv_store[0]
    swapped = swap(theirs(store))
    held = jnp.where(src % 2 == core, mine(store), swapped)
    pieces = lax.all_to_all(held.reshape(chips, slab // chips, slab), CHIP, 0, 0, tiled=True)
    piece = lax.dynamic_index_in_dim(pieces, src // 2, 0, keepdims=False)
    panel = lax.all_to_all(jnp.broadcast_to(piece[None], (chips,) + piece.shape), CHIP, 0, 0, tiled=True)
    panel = panel.reshape(slab, slab) * expand(mine(a_mask)).astype(jnp.bfloat16)

    columns = mine(acts).reshape(count, groups, slab).transpose(1, 0, 2)
    columns = lax.all_to_all(columns, GRP, 0, 0, tiled=True).reshape(tokens, slab)

    own, got = mine(out_grads), swap(theirs(out_grads))
    pair = jnp.concatenate([jnp.where(first, own, got), jnp.where(first, got, own)], axis=1)
    grads = gather_grp(pair).reshape(tokens, 2 * gcol)

    g_panels = [g_inv[l] * expand(g_mask[l]).astype(jnp.bfloat16) for l in range(2)]
    g_panels = jnp.stack(g_panels)
    g_own, g_got = mine(g_panels), swap(theirs(g_panels))

    weight_grad = lax.dot_general(
        columns, grads, (((0,), (0,)), ((), ())), preferred_element_type=F32
    ).astype(jnp.bfloat16)
    left = jnp.dot(panel, weight_grad, preferred_element_type=F32).astype(jnp.bfloat16)
    left_own = lax.dynamic_slice_in_dim(left, core * gcol, gcol, 1)
    left_got = lax.dynamic_slice_in_dim(left, other * gcol, gcol, 1)
    right_got = jnp.dot(left_got, g_got, preferred_element_type=F32).astype(jnp.bfloat16)
    right_own = jnp.dot(left_own, g_own, preferred_element_type=F32).astype(jnp.bfloat16)
    right_in = swap(right_got)

    rows = lax.dynamic_slice_in_dim(columns, chip_at * 2 * arows, 2 * arows, 1)
    a_gram = lax.dot_general(rows, columns, (((0,), (0,)), ((), ())), preferred_element_type=F32)
    a_gram = a_gram.reshape(2, arows, slab)
    a_own, a_in = mine(a_gram), swap(theirs(a_gram))
    blocks = grads.reshape(tokens, 2, gcol)
    part = lax.dynamic_slice_in_dim(blocks, grp_at * grows, grows, 2)
    g_gram = jnp.einsum("twr,twc->wrc", part, blocks, preferred_element_type=F32)
    gg_own, gg_in = mine(g_gram), swap(theirs(g_gram))

    def layered(own_layer, other_layer):
        return jnp.stack([jnp.where(first, own_layer, other_layer), jnp.where(first, other_layer, own_layer)])

    precond = layered(right_own, right_in)
    a_new = DECAY * a_factor + (1.0 - DECAY) * (layered(a_own, a_in) / tokens)
    g_new = DECAY * g_factor + (1.0 - DECAY) * layered(gg_own, gg_in)
    return precond, a_new, g_new


def solution(mesh):
    fine = Mesh(mesh.devices.reshape(4, 2, 2, 8, 2), ("y", "xl", "xh", "z", "core"))
    wide = ("xh", "z", "core")
    in_specs = (
        P(None, GRP, None),
        P(None, GRP, wide),
        P(None, wide, GRP),
        P(None, GRP, wide),
        P(wide, None, GRP, None),
        P(None, GRP, None),
        P(None, wide, None),
        P(None, wide, None),
        P(),
    )
    out_specs = (P(None, GRP, wide), P(None, wide, GRP), P(None, GRP, wide))
    return jax.shard_map(shards, mesh=fine, in_specs=in_specs, out_specs=out_specs, check_vma=False)
```

```python
import jax
import jax.numpy as jnp
from jax import lax
from jax.sharding import Mesh, PartitionSpec as P

TILE = 128
DECAY = 0.9
GRP = ("y", "xl")
CHIP = ("xh", "z")
F32 = jnp.float32
BF16 = jnp.bfloat16


def expand(mask):
    return jnp.repeat(jnp.repeat(mask, TILE, axis=0), TILE, axis=1)


def swap(x):
    return lax.ppermute(x, "core", [(0, 1), (1, 0)])


def from_offset(x, dy, dx):
    ny, nx = lax.axis_size("y"), lax.axis_size("xl")
    pairs = [
        (((y + dy) % ny) * nx + (x_ + dx) % nx, y * nx + x_) for y in range(ny) for x_ in range(nx)
    ]
    return lax.ppermute(x, GRP, pairs)


def shards(acts, out_grads, a_factor, g_factor, ainv_store, a_mask, g_inv, g_mask, owner):
    core = lax.axis_index("core")
    other = 1 - core
    first = core == 0
    grp_at = lax.axis_index(GRP)
    chip_at = lax.axis_index(CHIP)
    y_at, xl_at = lax.axis_index("y"), lax.axis_index("xl")
    ny, nx = lax.axis_size("y"), lax.axis_size("xl")
    groups = ny * nx
    chips = lax.axis_size(CHIP)
    count = acts.shape[1]
    slab = acts.shape[2] // groups
    gcol = out_grads.shape[2]
    arows = a_factor.shape[1]
    grows = g_factor.shape[1]
    tokens = count * groups

    def mine(x):
        return lax.dynamic_index_in_dim(x, core, 0, keepdims=False)

    def theirs(x):
        return lax.dynamic_index_in_dim(x, other, 0, keepdims=False)

    src = mine(owner)
    store = ainv_store[0]
    swapped = swap(theirs(store))
    held = jnp.where(src % 2 == core, mine(store), swapped)
    pieces = lax.all_to_all(held.reshape(chips, slab // chips, slab), CHIP, 0, 0, tiled=True)
    piece = lax.dynamic_index_in_dim(pieces, src // 2, 0, keepdims=False)
    panel = lax.all_to_all(jnp.broadcast_to(piece[None], (chips,) + piece.shape), CHIP, 0, 0, tiled=True)
    panel = panel.reshape(slab, slab) * expand(mine(a_mask)).astype(BF16)

    own, got = mine(out_grads), swap(theirs(out_grads))
    pair = jnp.concatenate([jnp.where(first, own, got), jnp.where(first, got, own)], axis=1)
    near = jnp.concatenate([pair, from_offset(pair, 0, 1)])
    grads = jnp.concatenate([near] + [from_offset(near, dy, 0) for dy in range(1, ny)])

    blocks = []
    for dy in range(ny):
        for dx in range(nx):
            to = ((y_at - dy) % ny) * nx + (xl_at - dx) % nx
            part = lax.dynamic_slice(acts, (core, 0, to * slab), (1, count, slab))[0]
            blocks.append(part if dy == dx == 0 else from_offset(part, dy, dx))
    columns = jnp.concatenate(blocks)

    g_panels = jnp.stack([g_inv[l] * expand(g_mask[l]).astype(BF16) for l in range(2)])
    g_own, g_got = mine(g_panels), swap(theirs(g_panels))

    weight_grad = lax.dot_general(
        columns, grads, (((0,), (0,)), ((), ())), preferred_element_type=F32
    ).astype(BF16)

    rows = lax.dynamic_slice_in_dim(columns, chip_at * 2 * arows, 2 * arows, 1)
    a_gram = lax.dot_general(rows, columns, (((0,), (0,)), ((), ())), preferred_element_type=F32)
    a_gram = a_gram.reshape(2, arows, slab)
    a_own, a_in = mine(a_gram), swap(theirs(a_gram))
    halves = [grads[:, :gcol], grads[:, gcol:]]
    g_gram = jnp.stack([
        lax.dot_general(
            lax.dynamic_slice_in_dim(h, grp_at * grows, grows, 1), h, (((0,), (0,)), ((), ())),
            preferred_element_type=F32,
        )
        for h in halves
    ])
    gg_own, gg_in = mine(g_gram), swap(theirs(g_gram))

    left = jnp.dot(panel, weight_grad, preferred_element_type=F32).astype(BF16)
    left_own = lax.dynamic_slice_in_dim(left, core * gcol, gcol, 1)
    left_got = lax.dynamic_slice_in_dim(left, other * gcol, gcol, 1)
    right_got = jnp.dot(left_got, g_got, preferred_element_type=F32).astype(BF16)
    right_own = jnp.dot(left_own, g_own, preferred_element_type=F32).astype(BF16)
    right_in = swap(right_got)

    def layered(own_layer, other_layer):
        return jnp.stack([jnp.where(first, own_layer, other_layer), jnp.where(first, other_layer, own_layer)])

    precond = layered(right_own, right_in)
    a_new = DECAY * a_factor + (1.0 - DECAY) * (layered(a_own, a_in) / tokens)
    g_new = DECAY * g_factor + (1.0 - DECAY) * layered(gg_own, gg_in)
    return precond, a_new, g_new


def solution(mesh):
    fine = Mesh(mesh.devices.reshape(4, 2, 2, 8, 2), ("y", "xl", "xh", "z", "core"))
    wide = ("xh", "z", "core")
    in_specs = (
        P(None, GRP, None),
        P(None, GRP, wide),
        P(None, wide, GRP),
        P(None, GRP, wide),
        P(wide, None, GRP, None),
        P(None, GRP, None),
        P(None, wide, None),
        P(None, wide, None),
        P(),
    )
    out_specs = (P(None, GRP, wide), P(None, wide, GRP), P(None, GRP, wide))
    return jax.shard_map(shards, mesh=fine, in_specs=in_specs, out_specs=out_specs, check_vma=False)
```

```python
import jax
import jax.numpy as jnp
from jax import lax
from jax.experimental import pallas as pl
from jax.experimental.pallas import tpu as pltpu
from jax.sharding import Mesh, PartitionSpec as P

TILE = 128
DECAY = 0.9
GRP = ("y", "xl")
CHIP = ("xh", "z")
F32 = jnp.float32
BF16 = jnp.bfloat16
VMEM = pl.BlockSpec(memory_space=pltpu.VMEM)
SMEM = pl.BlockSpec(memory_space=pltpu.SMEM)


def expand(mask):
    return jnp.repeat(jnp.repeat(mask, TILE, axis=0), TILE, axis=1)


def swap(x, axis="core"):
    return lax.ppermute(x, axis, [(0, 1), (1, 0)])


def shift(x, axis, step):
    size = lax.axis_size(axis)
    return lax.ppermute(x, axis, [(i, (i + step) % size) for i in range(size)])


def from_offset(x, dy, dx):
    ny, nx = lax.axis_size("y"), lax.axis_size("xl")
    pairs = [
        (((y + dy) % ny) * nx + (x_ + dx) % nx, y * nx + x_) for y in range(ny) for x_ in range(nx)
    ]
    return lax.ppermute(x, GRP, pairs)


def across(a, b):
    return lax.dot_general(a, b, (((0,), (0,)), ((), ())), preferred_element_type=F32)


def products(columns, near, g_got, g_own, arows, grows):
    pieces, steps = len(columns), len(near)
    count, slab = columns[0].shape
    span = count * pieces // steps
    gcol = g_own.shape[0]
    window = 2 * TILE

    def body(at, *refs):
        parts, n = refs[:pieces], refs[pieces : pieces + steps]
        gg, go, in_got, in_own, a_out, g_out, a, weight, gram = refs[pieces + steps :]
        core, chip, grp = at[0], at[1], at[2]
        for index, part in enumerate(parts):
            a[pl.ds(index * count, count), :] = part[...]

        def tok(step):
            return pl.ds(step * span, span)

        for half in range(2):
            cols = pl.ds(half * gcol, gcol)
            total = across(a[tok(0), :], n[0][:, cols])
            for step in range(1, steps):
                total += across(a[tok(step), :], n[step][:, cols])
            weight[half] = total.astype(BF16)
        in_got[...] = jnp.dot(weight[1 - core], gg[...], preferred_element_type=F32).astype(BF16)
        in_own[...] = jnp.dot(weight[core], go[...], preferred_element_type=F32).astype(BF16)

        row = chip * (2 * arows)
        start = jnp.minimum(row // TILE * TILE, slab - window)
        lhs = a[:, pl.ds(pl.multiple_of(start, TILE), window)]
        gram[...] = across(lhs, a[...])
        a_out[...] = gram[pl.ds(pl.multiple_of(row - start, 8), 2 * arows), :]
        row = grp * grows
        start = jnp.minimum(row // TILE * TILE, gcol - window)
        for half in range(2):
            total = None
            for step in range(steps):
                lhs = n[step][:, pl.ds(pl.multiple_of(half * gcol + start, TILE), window)]
                part = across(lhs, n[step][:, pl.ds(half * gcol, gcol)])
                total = part if total is None else total + part
            gram[:, pl.ds(0, gcol)] = total
            g_out[half] = gram[pl.ds(pl.multiple_of(row - start, 8), grows), pl.ds(0, gcol)]

    at = jnp.stack([lax.axis_index("core"), lax.axis_index(CHIP), lax.axis_index(GRP)])
    outs = (
        jax.ShapeDtypeStruct((slab, gcol), BF16),
        jax.ShapeDtypeStruct((slab, gcol), BF16),
        jax.ShapeDtypeStruct((2 * arows, slab), F32),
        jax.ShapeDtypeStruct((2, grows, gcol), F32),
    )
    return pl.pallas_call(
        body,
        out_shape=outs,
        in_specs=[SMEM] + [VMEM] * (pieces + steps + 2),
        out_specs=(VMEM,) * 4,
        scratch_shapes=[pltpu.VMEM((count * pieces, slab), BF16), pltpu.VMEM((2, slab, gcol), BF16), pltpu.VMEM((window, slab), F32)],
        cost_estimate=pl.CostEstimate(flops=3 * 10**9, bytes_accessed=8 * 10**6, transcendentals=0),
        compiler_params=pltpu.CompilerParams(vmem_limit_bytes=20 * 2**20),
    )(at.astype(jnp.int32), *columns, *near, g_got, g_own)


def outer(parts, offsets, inner, received=None):
    slab, gcol = inner.shape
    count = len(parts)

    def body(at, *refs):
        blocks, right, out = refs[:count], refs[count], refs[-1]
        for index, block in enumerate(blocks):
            rows = pl.ds(pl.multiple_of(at[index], 16), block.shape[0])
            value = jnp.dot(block[...], right[...], preferred_element_type=F32).astype(BF16)
            if received is None:
                out[rows, :] = value
            else:
                out[at[count], rows, :] = value
        if received is not None:
            out[1 - at[count]] = refs[count + 1][...]

    shape = (slab, gcol) if received is None else (2, slab, gcol)
    rest = () if received is None else (received,)
    at = jnp.stack(list(offsets) + [lax.axis_index("core")]).astype(jnp.int32)
    return pl.pallas_call(
        body,
        out_shape=jax.ShapeDtypeStruct(shape, BF16),
        in_specs=[SMEM] + [VMEM] * (count + 1 + len(rest)),
        out_specs=VMEM,
        cost_estimate=pl.CostEstimate(flops=10**9, bytes_accessed=3 * 10**6, transcendentals=0),
        compiler_params=pltpu.CompilerParams(vmem_limit_bytes=12 * 2**20),
    )(at, *parts, inner, *rest)


def shards(acts, out_grads, a_factor, g_factor, ainv_store, a_mask, g_inv, g_mask, owner):
    core = lax.axis_index("core")
    other = 1 - core
    first = core == 0
    y_at, xl_at = lax.axis_index("y"), lax.axis_index("xl")
    ny, nx = lax.axis_size("y"), lax.axis_size("xl")
    depth = lax.axis_size("z")
    groups = lax.axis_size(GRP)
    count = acts.shape[1]
    slab = acts.shape[2] // groups
    arows = a_factor.shape[1]
    grows = g_factor.shape[1]
    tokens = count * groups
    rows = slab // depth

    def mine(x):
        return lax.dynamic_index_in_dim(x, core, 0, keepdims=False)

    def theirs(x):
        return lax.dynamic_index_in_dim(x, other, 0, keepdims=False)

    src = mine(owner)
    store = ainv_store[0]
    kept, sent = lax.optimization_barrier((mine(store), theirs(store)))
    swapped = swap(sent)
    held = jnp.where(src % 2 == core, kept, swapped)
    pieces = lax.all_to_all(held.reshape(depth, rows, slab), "z", 0, 0, tiled=True)

    own, got = mine(out_grads), swap(theirs(out_grads))
    pair = jnp.concatenate([jnp.where(first, own, got), jnp.where(first, got, own)], axis=1)
    near = jnp.concatenate([pair, from_offset(pair, 0, 1)])
    near = [near] + [from_offset(near, dy, 0) for dy in range(1, ny)]

    ready = jnp.isfinite(swapped[0, 0])
    columns = []
    for dy in range(ny):
        for dx in range(nx):
            to = ((y_at - dy) % ny) * nx + (xl_at - dx) % nx
            to = jnp.where(ready, to, 0)
            part = lax.dynamic_slice(acts, (core, 0, to * slab), (1, count, slab))[0]
            columns.append(part if dy == dx == 0 else from_offset(part, dy, dx))

    tiles = expand(mine(a_mask)).astype(BF16)
    tiles = lax.optimization_barrier(lax.dynamic_slice_in_dim(tiles, lax.axis_index("z") * rows, rows, 0))
    piece = lax.dynamic_index_in_dim(pieces, src // 2 % depth, 0, keepdims=False) * tiles
    piece = jnp.where(src // 2 // depth == lax.axis_index("xh"), piece, swap(piece, "xh"))
    here = sum(x[:8, :TILE] for x in columns[1:]) + near[0][-8:, :TILE]
    piece = jnp.where(jnp.isfinite(here[0, 0]), piece, 0)
    panel = lax.all_to_all(jnp.broadcast_to(piece[None], (depth,) + piece.shape), "z", 0, 0, tiled=True)
    parts, offsets = [panel.reshape(slab, slab)], [0 * core]

    g_panels = jnp.stack([g_inv[l] * expand(g_mask[l]).astype(BF16) for l in range(2)])
    g_own, g_got = mine(g_panels), swap(theirs(g_panels))

    inner_got, inner_own, a_gram, g_gram = products(columns, near, g_got, g_own, arows, grows)
    a_gram = a_gram.reshape(2, arows, slab)
    a_own, a_in = mine(a_gram), swap(theirs(a_gram))
    gg_own, gg_in = mine(g_gram), swap(theirs(g_gram))
    received = swap(outer(parts, offsets, inner_got))
    precond = outer(parts, offsets, inner_own, received)

    def layered(own_layer, other_layer):
        return jnp.stack([jnp.where(first, own_layer, other_layer), jnp.where(first, other_layer, own_layer)])

    a_new = DECAY * a_factor + (1.0 - DECAY) * (layered(a_own, a_in) / tokens)
    g_new = DECAY * g_factor + (1.0 - DECAY) * layered(gg_own, gg_in)
    return precond, a_new, g_new


def solution(mesh):
    fine = Mesh(mesh.devices.reshape(4, 2, 2, 8, 2), ("y", "xl", "xh", "z", "core"))
    wide = ("xh", "z", "core")
    in_specs = (
        P(None, GRP, None),
        P(None, GRP, wide),
        P(None, wide, GRP),
        P(None, GRP, wide),
        P(wide, None, GRP, None),
        P(None, GRP, None),
        P(None, wide, None),
        P(None, wide, None),
        P(),
    )
    out_specs = (P(None, GRP, wide), P(None, wide, GRP), P(None, GRP, wide))
    return jax.shard_map(shards, mesh=fine, in_specs=in_specs, out_specs=out_specs, check_vma=False)
```

```python
import jax
import jax.numpy as jnp
from jax import lax
from jax.experimental import pallas as pl
from jax.experimental.pallas import tpu as pltpu
from jax.sharding import Mesh, PartitionSpec as P

TILE = 128
DECAY = 0.9
GRP = ("y", "xl")
CHIP = ("xh", "z")
F32 = jnp.float32
BF16 = jnp.bfloat16
VMEM = pl.BlockSpec(memory_space=pltpu.VMEM)
ANY = pl.BlockSpec(memory_space=pl.ANY)
SMEM = pl.BlockSpec(memory_space=pltpu.SMEM)


def expand(mask):
    return jnp.repeat(jnp.repeat(mask, TILE, axis=0), TILE, axis=1)


def swap(x, axis="core"):
    return lax.ppermute(x, axis, [(0, 1), (1, 0)])


def shift(x, axis, step):
    size = lax.axis_size(axis)
    return lax.ppermute(x, axis, [(i, (i + step) % size) for i in range(size)])


def from_offset(x, dy, dx):
    ny, nx = lax.axis_size("y"), lax.axis_size("xl")
    pairs = [
        (((y + dy) % ny) * nx + (x_ + dx) % nx, y * nx + x_) for y in range(ny) for x_ in range(nx)
    ]
    return lax.ppermute(x, GRP, pairs)


def across(a, b):
    return lax.dot_general(a, b, (((0,), (0,)), ((), ())), preferred_element_type=F32)


def products(columns, near, g_got, g_own, arows, grows, after):
    pieces, steps = len(columns), len(near)
    count, slab = columns[0].shape
    span = count * pieces // steps
    gcol = g_own.shape[0]
    window = 2 * TILE

    def body(at, *refs):
        parts, n = refs[:pieces], refs[pieces : pieces + steps]
        gg, go, _, in_got, in_own, a_out, g_out, a, weight, gram = refs[pieces + steps :]
        core, chip, grp = at[0], at[1], at[2]
        for index, part in enumerate(parts):
            a[pl.ds(index * count, count), :] = part[...]

        def tok(step):
            return pl.ds(step * span, span)

        for half in range(2):
            cols = pl.ds(half * gcol, gcol)
            total = across(a[tok(0), :], n[0][:, cols])
            for step in range(1, steps):
                total += across(a[tok(step), :], n[step][:, cols])
            weight[half] = total.astype(BF16)
        in_got[...] = jnp.dot(weight[1 - core], gg[...], preferred_element_type=F32).astype(BF16)
        in_own[...] = jnp.dot(weight[core], go[...], preferred_element_type=F32).astype(BF16)

        row = chip * (2 * arows)
        start = jnp.minimum(row // TILE * TILE, slab - window)
        lhs = a[:, pl.ds(pl.multiple_of(start, TILE), window)]
        gram[...] = across(lhs, a[...])
        a_out[...] = gram[pl.ds(pl.multiple_of(row - start, 8), 2 * arows), :]
        row = grp * grows
        start = jnp.minimum(row // TILE * TILE, gcol - window)
        for half in range(2):
            total = None
            for step in range(steps):
                lhs = n[step][:, pl.ds(pl.multiple_of(half * gcol + start, TILE), window)]
                part = across(lhs, n[step][:, pl.ds(half * gcol, gcol)])
                total = part if total is None else total + part
            gram[:, pl.ds(0, gcol)] = total
            g_out[half] = gram[pl.ds(pl.multiple_of(row - start, 8), grows), pl.ds(0, gcol)]

    at = jnp.stack([lax.axis_index("core"), lax.axis_index(CHIP), lax.axis_index(GRP)])
    outs = (
        jax.ShapeDtypeStruct((slab, gcol), BF16),
        jax.ShapeDtypeStruct((slab, gcol), BF16),
        jax.ShapeDtypeStruct((2 * arows, slab), F32),
        jax.ShapeDtypeStruct((2, grows, gcol), F32),
    )
    return pl.pallas_call(
        body,
        out_shape=outs,
        in_specs=[SMEM] + [VMEM] * (pieces + steps + 2) + [ANY],
        out_specs=(VMEM,) * 4,
        scratch_shapes=[pltpu.VMEM((count * pieces, slab), BF16), pltpu.VMEM((2, slab, gcol), BF16), pltpu.VMEM((window, slab), F32)],
        cost_estimate=pl.CostEstimate(flops=3 * 10**9, bytes_accessed=8 * 10**6, transcendentals=0),
        compiler_params=pltpu.CompilerParams(vmem_limit_bytes=20 * 2**20),
    )(at.astype(jnp.int32), *columns, *near, g_got, g_own, after)


def outer(parts, first, second):
    rows, slab = sum(part.shape[0] for part in parts), parts[0].shape[1]

    def body(*refs):
        one, two, out_one, out_two, left = refs[len(parts) :]
        row = 0
        for part in refs[: len(parts)]:
            left[pl.ds(row, part.shape[0]), :] = part[...]
            row += part.shape[0]
        out_one[...] = jnp.dot(left[...], one[...], preferred_element_type=F32).astype(BF16)
        out_two[...] = jnp.dot(left[...], two[...], preferred_element_type=F32).astype(BF16)

    return pl.pallas_call(
        body,
        out_shape=(jax.ShapeDtypeStruct((rows, first.shape[1]), BF16),) * 2,
        in_specs=[VMEM] * (len(parts) + 2),
        out_specs=(VMEM,) * 2,
        scratch_shapes=[pltpu.VMEM((rows, slab), BF16)],
        cost_estimate=pl.CostEstimate(flops=10**9, bytes_accessed=10**6, transcendentals=0),
        compiler_params=pltpu.CompilerParams(vmem_limit_bytes=16 * 2**20),
    )(*parts, first, second)


def finish(own, received, offsets, step):
    slab, gcol = step * len(offsets), own[0].shape[1]
    count = len(own)

    def body(at, *refs):
        core, out = at[len(offsets)], refs[-1]
        for layer, blocks in ((core, refs[:count]), (1 - core, refs[count:-1])):
            index = 0
            for block in blocks:
                for row in range(0, block.shape[0], step):
                    rows = pl.ds(pl.multiple_of(at[index], 16), step)
                    out[layer, rows, :] = block[pl.ds(row, step), :]
                    index += 1

    at = jnp.stack(list(offsets) + [lax.axis_index("core")]).astype(jnp.int32)
    return pl.pallas_call(
        body,
        out_shape=jax.ShapeDtypeStruct((2, slab, gcol), BF16),
        in_specs=[SMEM] + [VMEM] * (2 * count),
        out_specs=VMEM,
        cost_estimate=pl.CostEstimate(flops=0, bytes_accessed=3 * 10**6, transcendentals=0),
        compiler_params=pltpu.CompilerParams(vmem_limit_bytes=12 * 2**20),
    )(at, *own, *received)


def shards(acts, out_grads, a_factor, g_factor, ainv_store, a_mask, g_inv, g_mask, owner):
    core = lax.axis_index("core")
    other = 1 - core
    first = core == 0
    y_at, xl_at = lax.axis_index("y"), lax.axis_index("xl")
    ny, nx = lax.axis_size("y"), lax.axis_size("xl")
    depth = lax.axis_size("z")
    groups = lax.axis_size(GRP)
    count = acts.shape[1]
    slab = acts.shape[2] // groups
    arows = a_factor.shape[1]
    grows = g_factor.shape[1]
    tokens = count * groups
    rows = slab // depth

    def mine(x):
        return lax.dynamic_index_in_dim(x, core, 0, keepdims=False)

    def theirs(x):
        return lax.dynamic_index_in_dim(x, other, 0, keepdims=False)

    src = mine(owner)
    store = ainv_store[0]
    kept, sent = lax.optimization_barrier((mine(store), theirs(store)))
    swapped = swap(sent)
    held = jnp.where(src % 2 == core, kept, swapped)
    pieces = lax.all_to_all(held.reshape(depth, rows, slab), "z", 0, 0, tiled=True)

    own, got = mine(out_grads), swap(theirs(out_grads))
    pair = jnp.concatenate([jnp.where(first, own, got), jnp.where(first, got, own)], axis=1)
    near = jnp.concatenate([pair, from_offset(pair, 0, 1)])
    near = [near]

    ready = jnp.isfinite(swapped[0, 0])
    columns = []
    for dy in range(ny):
        for dx in range(nx):
            to = ((y_at - dy) % ny) * nx + (xl_at - dx) % nx
            to = jnp.where(ready, to, 0)
            part = lax.dynamic_slice(acts, (core, 0, to * slab), (1, count, slab))[0]
            columns.append(part if dy == dx == 0 else from_offset(part, dy, dx))

    tiles = expand(mine(a_mask)).astype(BF16)
    tiles = lax.dynamic_slice_in_dim(tiles, lax.axis_index("z") * rows, rows, 0)
    tiles = lax.optimization_barrier(tiles)
    picked = lax.dynamic_index_in_dim(pieces, src // 2 % depth, 0, keepdims=False) * tiles
    piece = jnp.where(src // 2 // depth == lax.axis_index("xh"), picked, swap(picked, "xh"))

    here = sum(x[:8, :TILE] for x in columns[1:]) + near[0][-8:, :TILE]
    piece = jnp.where(jnp.isfinite(here[0, 0]), piece, 0)
    z_at = lax.axis_index("z")
    parts, offsets = [piece], [z_at]
    up = down = piece
    for step in range(1, depth // 2):
        up, down = shift(up, "z", 1), shift(down, "z", -1)
        parts += [up, down]
        offsets += [(z_at - step) % depth, (z_at + step) % depth]
    half = rows // 2
    parts += [shift(up[:half], "z", 1), shift(down[half:], "z", -1)]
    offsets = [at * rows for at in offsets + [(z_at + depth // 2) % depth]]
    near += [from_offset(near[0], dy, 0) for dy in range(1, ny)]

    g_panels = jnp.stack([g_inv[l] * expand(g_mask[l]).astype(BF16) for l in range(2)])
    g_own, g_got = mine(g_panels), swap(theirs(g_panels))

    inner_got, inner_own, a_gram, g_gram = products(columns, near, g_got, g_own, arows, grows, parts[3])
    a_gram = a_gram.reshape(2, arows, slab)
    a_own, a_in = mine(a_gram), swap(theirs(a_gram))
    gg_own, gg_in = mine(g_gram), swap(theirs(g_gram))
    own, received = [], []
    for group in (parts[:-2], parts[-2:]):
        got_rows, own_rows = outer(group, inner_got, inner_own)
        own.append(own_rows)
        received.append(swap(got_rows))
    precond = finish(own, received, offsets, rows)

    def layered(own_layer, other_layer):
        return jnp.stack([jnp.where(first, own_layer, other_layer), jnp.where(first, other_layer, own_layer)])

    a_new = DECAY * a_factor + (1.0 - DECAY) * (layered(a_own, a_in) / tokens)
    g_new = DECAY * g_factor + (1.0 - DECAY) * layered(gg_own, gg_in)
    return precond, a_new, g_new


def solution(mesh):
    fine = Mesh(mesh.devices.reshape(4, 2, 2, 8, 2), ("y", "xl", "xh", "z", "core"))
    wide = ("xh", "z", "core")
    in_specs = (
        P(None, GRP, None),
        P(None, GRP, wide),
        P(None, wide, GRP),
        P(None, GRP, wide),
        P(wide, None, GRP, None),
        P(None, GRP, None),
        P(None, wide, None),
        P(None, wide, None),
        P(),
    )
    out_specs = (P(None, GRP, wide), P(None, wide, GRP), P(None, GRP, wide))
    return jax.shard_map(shards, mesh=fine, in_specs=in_specs, out_specs=out_specs, check_vma=False)
```

```python
import jax
import jax.numpy as jnp
from jax import lax
from jax.experimental import pallas as pl
from jax.experimental.pallas import tpu as pltpu
from jax.sharding import Mesh, PartitionSpec as P

TILE = 128
DECAY = 0.9
GRP = ("y", "xl")
CHIP = ("xh", "z")
F32 = jnp.float32
BF16 = jnp.bfloat16
VMEM = pl.BlockSpec(memory_space=pltpu.VMEM)
ANY = pl.BlockSpec(memory_space=pl.ANY)
SMEM = pl.BlockSpec(memory_space=pltpu.SMEM)


def expand(mask):
    return jnp.repeat(jnp.repeat(mask, TILE, axis=0), TILE, axis=1)


def swap(x, axis="core"):
    return lax.ppermute(x, axis, [(0, 1), (1, 0)])


def shift(x, axis, step):
    size = lax.axis_size(axis)
    return lax.ppermute(x, axis, [(i, (i + step) % size) for i in range(size)])


def from_offset(x, dy, dx):
    ny, nx = lax.axis_size("y"), lax.axis_size("xl")
    pairs = [
        (((y + dy) % ny) * nx + (x_ + dx) % nx, y * nx + x_) for y in range(ny) for x_ in range(nx)
    ]
    return lax.ppermute(x, GRP, pairs)


def across(a, b):
    return lax.dot_general(a, b, (((0,), (0,)), ((), ())), preferred_element_type=F32)


def products(columns, near, g_got, g_own, arows, grows, after):
    pieces, steps = len(columns), len(near)
    count, slab = columns[0].shape
    span = count * pieces // steps
    gcol = g_own.shape[0]
    window = 2 * TILE

    def body(at, *refs):
        parts, n = refs[:pieces], refs[pieces : pieces + steps]
        gg, go, _, in_got, in_own, a_out, g_out, a, weight, gram = refs[pieces + steps :]
        core, chip, grp = at[0], at[1], at[2]
        for index, part in enumerate(parts):
            a[pl.ds(index * count, count), :] = part[...]

        def tok(step):
            return pl.ds(step * span, span)

        total = across(a[tok(0), :], n[0][...])
        for step in range(1, steps):
            total += across(a[tok(step), :], n[step][...])
        total = total.astype(BF16)
        for half in range(2):
            weight[half] = total[:, half * gcol : (half + 1) * gcol]
        in_got[...] = jnp.dot(weight[1 - core], gg[...], preferred_element_type=F32).astype(BF16)
        in_own[...] = jnp.dot(weight[core], go[...], preferred_element_type=F32).astype(BF16)

        row = chip * (2 * arows)
        start = jnp.minimum(row // TILE * TILE, slab - window)
        lhs = a[:, pl.ds(pl.multiple_of(start, TILE), window)]
        gram[...] = across(lhs, a[...])
        a_out[...] = gram[pl.ds(pl.multiple_of(row - start, 8), 2 * arows), :]
        row = grp * grows
        start = jnp.minimum(row // TILE * TILE, gcol - window)
        for half in range(2):
            total = None
            for step in range(steps):
                lhs = n[step][:, pl.ds(pl.multiple_of(half * gcol + start, TILE), window)]
                part = across(lhs, n[step][:, pl.ds(half * gcol, gcol)])
                total = part if total is None else total + part
            gram[:, pl.ds(0, gcol)] = total
            g_out[half] = gram[pl.ds(pl.multiple_of(row - start, 8), grows), pl.ds(0, gcol)]

    at = jnp.stack([lax.axis_index("core"), lax.axis_index(CHIP), lax.axis_index(GRP)])
    outs = (
        jax.ShapeDtypeStruct((slab, gcol), BF16),
        jax.ShapeDtypeStruct((slab, gcol), BF16),
        jax.ShapeDtypeStruct((2 * arows, slab), F32),
        jax.ShapeDtypeStruct((2, grows, gcol), F32),
    )
    return pl.pallas_call(
        body,
        out_shape=outs,
        in_specs=[SMEM] + [VMEM] * (pieces + steps + 2) + [ANY],
        out_specs=(VMEM,) * 4,
        scratch_shapes=[pltpu.VMEM((count * pieces, slab), BF16), pltpu.VMEM((2, slab, gcol), BF16), pltpu.VMEM((window, slab), F32)],
        cost_estimate=pl.CostEstimate(flops=3 * 10**9, bytes_accessed=8 * 10**6, transcendentals=0),
        compiler_params=pltpu.CompilerParams(vmem_limit_bytes=20 * 2**20),
    )(at.astype(jnp.int32), *columns, *near, g_got, g_own, after)


def outer(parts, first, second, along=()):
    rows, slab = sum(part.shape[0] for part in parts), parts[0].shape[1]
    extra = len(along)

    def body(*refs):
        one, two, *rest = refs[len(parts) :]
        passed, (out_one, out_two), copies, left = rest[:extra], rest[extra : extra + 2], rest[extra + 2 : -1], rest[-1]
        for source, out in zip(passed, copies):
            out[...] = source[...]
        row = 0
        for part in refs[: len(parts)]:
            left[pl.ds(row, part.shape[0]), :] = part[...]
            row += part.shape[0]
        out_one[...] = jnp.dot(left[...], one[...], preferred_element_type=F32).astype(BF16)
        out_two[...] = jnp.dot(left[...], two[...], preferred_element_type=F32).astype(BF16)

    return pl.pallas_call(
        body,
        out_shape=[jax.ShapeDtypeStruct((rows, first.shape[1]), BF16)] * 2
        + [jax.ShapeDtypeStruct(x.shape, x.dtype) for x in along],
        in_specs=[VMEM] * (len(parts) + 2 + extra),
        out_specs=[VMEM] * (2 + extra),
        scratch_shapes=[pltpu.VMEM((rows, slab), BF16)],
        cost_estimate=pl.CostEstimate(flops=10**9, bytes_accessed=10**6, transcendentals=0),
        compiler_params=pltpu.CompilerParams(vmem_limit_bytes=16 * 2**20),
    )(*parts, first, second, *along)


def finish(own, received, offsets, step):
    slab, gcol = step * len(offsets), own[0].shape[1]
    count = len(own)

    def body(at, *refs):
        core, out = at[len(offsets)], refs[-1]
        for layer, blocks in ((core, refs[:count]), (1 - core, refs[count:-1])):
            index = 0
            for block in blocks:
                for row in range(0, block.shape[0], step):
                    rows = pl.ds(pl.multiple_of(at[index], 16), step)
                    out[layer, rows, :] = block[pl.ds(row, step), :]
                    index += 1

    at = jnp.stack(list(offsets) + [lax.axis_index("core")]).astype(jnp.int32)
    return pl.pallas_call(
        body,
        out_shape=jax.ShapeDtypeStruct((2, slab, gcol), BF16),
        in_specs=[SMEM] + [VMEM] * (2 * count),
        out_specs=VMEM,
        cost_estimate=pl.CostEstimate(flops=0, bytes_accessed=3 * 10**6, transcendentals=0),
        compiler_params=pltpu.CompilerParams(vmem_limit_bytes=12 * 2**20),
    )(at, *own, *received)


def masked(blocks, mask):
    layers, tiles = mask.shape[0], mask.shape[1]

    def body(keep, block, out):
        for layer in range(layers):
            for i in range(tiles):
                for j in range(tiles):
                    at = (layer, pl.ds(i * TILE, TILE), pl.ds(j * TILE, TILE))
                    out[at] = block[at] * keep[layer, i, j].astype(F32).astype(BF16)

    return pl.pallas_call(
        body,
        out_shape=jax.ShapeDtypeStruct(blocks.shape, blocks.dtype),
        in_specs=[SMEM, VMEM],
        out_specs=VMEM,
        cost_estimate=pl.CostEstimate(flops=10**5, bytes_accessed=10**6, transcendentals=0),
        compiler_params=pltpu.CompilerParams(vmem_limit_bytes=4 * 2**20),
    )(mask, blocks)


def shards(acts, out_grads, a_factor, g_factor, ainv_store, a_mask, g_inv, g_mask, owner):
    core = lax.axis_index("core")
    other = 1 - core
    first = core == 0
    y_at, xl_at = lax.axis_index("y"), lax.axis_index("xl")
    ny, nx = lax.axis_size("y"), lax.axis_size("xl")
    depth = lax.axis_size("z")
    groups = lax.axis_size(GRP)
    count = acts.shape[1]
    slab = acts.shape[2] // groups
    arows = a_factor.shape[1]
    grows = g_factor.shape[1]
    tokens = count * groups
    rows = slab // depth

    def mine(x):
        return lax.dynamic_index_in_dim(x, core, 0, keepdims=False)

    def theirs(x):
        return lax.dynamic_index_in_dim(x, other, 0, keepdims=False)

    src = mine(owner)
    store = ainv_store[0]
    kept, sent = lax.optimization_barrier((mine(store), theirs(store)))
    swapped = swap(sent)
    held = jnp.where(src % 2 == core, kept, swapped)
    pieces = lax.all_to_all(held.reshape(depth, rows, slab), "z", 0, 0, tiled=True)

    own, got = mine(out_grads), swap(theirs(out_grads))
    pair = jnp.concatenate([jnp.where(first, own, got), jnp.where(first, got, own)], axis=1)
    near = jnp.concatenate([pair, from_offset(pair, 0, 1)])
    near = [near]

    ready = jnp.isfinite(swapped[0, 0])
    columns = []
    for dy in range(ny):
        for dx in range(nx):
            to = ((y_at - dy) % ny) * nx + (xl_at - dx) % nx
            to = jnp.where(ready, to, 0)
            part = lax.dynamic_slice(acts, (core, 0, to * slab), (1, count, slab))[0]
            columns.append(part if dy == dx == 0 else from_offset(part, dy, dx))

    tiles = expand(mine(a_mask)).astype(BF16)
    tiles = lax.dynamic_slice_in_dim(tiles, lax.axis_index("z") * rows, rows, 0)
    tiles = lax.optimization_barrier(tiles)
    picked = lax.dynamic_index_in_dim(pieces, src // 2 % depth, 0, keepdims=False) * tiles
    piece = jnp.where(src // 2 // depth == lax.axis_index("xh"), picked, swap(picked, "xh"))

    here = sum(x[:8, :TILE] for x in columns[1:]) + near[0][-8:, :TILE]
    piece = jnp.where(jnp.isfinite(here[0, 0]), piece, 0)
    z_at = lax.axis_index("z")
    parts, offsets = [piece], [z_at]
    up = down = piece
    for step in range(1, depth // 2):
        up, down = shift(up, "z", 1), shift(down, "z", -1)
        parts += [up, down]
        offsets += [(z_at - step) % depth, (z_at + step) % depth]
    half = rows // 2
    parts += [shift(up[:half], "z", 1), shift(down[half:], "z", -1)]
    offsets = [at * rows for at in offsets + [(z_at + depth // 2) % depth]]
    near += [from_offset(near[0], dy, 0) for dy in range(1, ny)]

    g_panels = masked(g_inv, g_mask)
    g_own, g_got = mine(g_panels), swap(theirs(g_panels))

    inner_got, inner_own, a_gram, g_gram = products(columns, near, g_got, g_own, arows, grows, parts[3])
    got_rows, own_rows = outer(parts[:-2], inner_got, inner_own)
    last_got, last_own, a_gram, g_gram = outer(parts[-2:], inner_got, inner_own, (a_gram, g_gram))
    own, received = [own_rows, last_own], [swap(got_rows), swap(last_got)]
    a_gram = a_gram.reshape(2, arows, slab)
    a_own, a_in = mine(a_gram), swap(theirs(a_gram))
    gg_own, gg_in = mine(g_gram), swap(theirs(g_gram))
    precond = finish(own, received, offsets, rows)

    def layered(own_layer, other_layer):
        return jnp.stack([jnp.where(first, own_layer, other_layer), jnp.where(first, other_layer, own_layer)])

    a_new = DECAY * a_factor + (1.0 - DECAY) * (layered(a_own, a_in) / tokens)
    g_new = DECAY * g_factor + (1.0 - DECAY) * layered(gg_own, gg_in)
    return precond, a_new, g_new


def solution(mesh):
    fine = Mesh(mesh.devices.reshape(4, 2, 2, 8, 2), ("y", "xl", "xh", "z", "core"))
    wide = ("xh", "z", "core")
    in_specs = (
        P(None, GRP, None),
        P(None, GRP, wide),
        P(None, wide, GRP),
        P(None, GRP, wide),
        P(wide, None, GRP, None),
        P(None, GRP, None),
        P(None, wide, None),
        P(None, wide, None),
        P(),
    )
    out_specs = (P(None, GRP, wide), P(None, wide, GRP), P(None, GRP, wide))
    return jax.shard_map(shards, mesh=fine, in_specs=in_specs, out_specs=out_specs, check_vma=False)
```
